32 devices in a mesh: section: 16 (over z, y, core), seg: 2 (over x).
Axes of the slice: x: 2, y: 2, z: 4, core: 2. Of those that a mesh axis runs over, the one named last changes fastest.
Arguments:
- passage_word_codes: int32 [2, 256], P('seg'), may hold values from 0 to 16383
- word_vector_lookup: bfloat16 [16384, 2048], P('section'), may hold values from -6 to 6
- hidden_inputs: bfloat16 [2, 2048, 2048], P('seg', 'section'), may hold values from -6 to 6
- memory_blocks: bfloat16 [2, 2048, 2048], P('seg', 'section'), may hold values from -6 to 6
- asking_matrix: bfloat16 [16, 2048, 512], P('section'), may hold values from -0.125 to 0.125
- matching_matrix: bfloat16 [16, 2048, 512], P('section'), may hold values from -0.125 to 0.125
- content_matrix: bfloat16 [16, 2048, 512], P('section'), may hold values from -0.125 to 0.125
- projection_back_matrix: bfloat16 [16, 512, 2048], P('section'), may hold values from -0.75 to 0.75
- word_scale_factor: float32 [8, 2048], replicated, may hold values from 0.25 to 1.75
- memory_scale_factor: float32 [8, 2048], replicated, may hold values from 0.25 to 1.75
- memory_retention_share: float32 [8, 2048], replicated, may hold values from 0.1 to 0.9
- score_scaling: float32 [16, 4], P('section'), may hold values from 0.5 to 4, as said below
Outputs:
- hidden: bfloat16 [2, 2048, 2048], P('seg', 'section')
- new_states: bfloat16 [2, 2048, 2048], P('seg', 'section')
The draws below stay inside these ranges and needn't reach their ends.
Inputs may be any that keep to these rules, and one draw needn't show every extreme that they name: `score_scaling`: positive score scales.
All inputs are finite; a program needn't handle non-finite values.
Results may differ from the reference program's by a relative error of at most 0.028.
The reference program's roundings to bfloat16 on the way count: a program that leaves them out, or rounds other values in their place, can miss the bound.
Values may be sent and summed in bfloat16 or wider, within the bound.
A program may use at most 64 MiB of HBM per device.

```python
import math
import jax
import jax.numpy as jnp
import numpy as np
from jax import lax

D = 2048
HEADS = 8
HEAD_DIM = 128
MEMORY_LINES = 256
VOCAB = 16384
SEG_TOK = 256
DEPTH_TOTAL = 8
N_SEG = 2


def draw_score_scaling(key, part):
    spread = jax.random.uniform(key, (2 * DEPTH_TOTAL, HEADS // 2), jnp.float32)
    low_end = 0.5
    high_end = 2.0
    return jnp.exp(jnp.log(low_end) + spread * (jnp.log(high_end) - jnp.log(low_end)))


def touch_ends(values, own_key, smallest, top_value):
    extent = values.shape
    index_at = [jax.random.randint(jax.random.fold_in(own_key, axis), (), 0, extent[axis]) for axis in range(len(extent))]
    values = values.at[tuple(index_at)].set(smallest)
    longest = extent.index(max(extent))
    index_at[longest] = (index_at[longest] + 1) % extent[longest]
    return values.at[tuple(index_at)].set(top_value)


def steps_of(key, dims, shards, low, high):
    factor_of, own = 1.0, jax.random.fold_in(key, 6)
    for dim, shards_of in shards:
        heights = jnp.exp(jax.random.uniform(jax.random.fold_in(own, dim), (shards_of,), jnp.float32, low / len(shards), high / len(shards)))
        factor_of = factor_of * jnp.repeat(heights, dims[dim] // shards_of).reshape([-1 if axis == dim else 1 for axis in range(len(dims))])
    return factor_of


def cumulative_ranks(amount, slope):
    portions = [(1 << 20) // math.isqrt(grade ** slope) + 1 for grade in range(1, amount + 1)]
    scale = 1 + sum(portions) // (1 << 30)
    return np.cumsum(np.array([max(1, weight // scale) for weight in portions]))


def skewed_ids(rng, dims, count, skew):
    table = cumulative_ranks(count, skew)
    ticket = jax.random.randint(jax.random.fold_in(rng, 1), dims, 0, int(table[count - 1]))
    standing = jnp.searchsorted(jnp.asarray(table, jnp.int32), ticket, side="right")
    return jax.random.permutation(jax.random.fold_in(rng, 2), count)[standing].astype(jnp.int32)


def gaussian(own_key, dims, scale, reach, split=(), held_as=jnp.bfloat16):
    values = jax.random.normal(own_key, dims, jnp.float32) * scale
    if len(split) > 0:
        values = steps_of(own_key, dims, split, -0.22, 0.18) * values
    return jnp.clip(values, min=-reach, max=reach).astype(held_as)


def setup_inputs(seed: int = 0) -> dict:
    streams_of = jax.random.split(jax.random.key(seed), 13)
    passage_word_codes = touch_ends(skewed_ids(streams_of[0], (N_SEG, SEG_TOK), VOCAB, 2), jax.random.fold_in(streams_of[0], 3), 0, VOCAB - 1).astype(jnp.int32)
    word_vector_lookup = gaussian(streams_of[1], (VOCAB, D), 1.0, 6.0, ((0, 16),))
    hidden_inputs = gaussian(streams_of[2], (N_SEG, DEPTH_TOTAL * SEG_TOK, D), 1.0, 6.0, ((0, 2), (1, 16)))
    memory_blocks = gaussian(streams_of[3], (N_SEG, DEPTH_TOTAL * MEMORY_LINES, D), 1.0, 6.0, ((0, 2), (1, 16)))
    asking_matrix = gaussian(streams_of[4], (2 * DEPTH_TOTAL, D, HEADS // 2 * HEAD_DIM), D ** -0.5, 0.125, ((0, 16),))
    matching_matrix = gaussian(streams_of[5], (2 * DEPTH_TOTAL, D, HEADS // 2 * HEAD_DIM), D ** -0.5, 0.125, ((0, 16),))
    content_matrix = gaussian(streams_of[6], (2 * DEPTH_TOTAL, D, HEADS // 2 * HEAD_DIM), D ** -0.5, 0.125, ((0, 16),))
    projection_back_matrix = gaussian(streams_of[7], (2 * DEPTH_TOTAL, HEADS // 2 * HEAD_DIM, D), (HEADS * HEAD_DIM // 16) ** -0.5, 0.75, ((0, 16),))
    word_scale_factor = jnp.clip(1.0 + 0.15 * jax.random.normal(streams_of[8], (DEPTH_TOTAL, D), jnp.float32), 0.25, 1.75)
    memory_scale_factor = jnp.clip(1.0 + 0.15 * jax.random.normal(streams_of[9], (DEPTH_TOTAL, D), jnp.float32), 0.25, 1.75)
    memory_retention_share = jnp.clip(jax.random.uniform(streams_of[10], (DEPTH_TOTAL, D), jnp.float32, 0.1, 0.9), 0.1, 0.9)
    score_scaling = draw_score_scaling(jax.random.fold_in(streams_of[12], 71), 0)
    return dict(passage_word_codes=passage_word_codes, word_vector_lookup=word_vector_lookup, hidden_inputs=hidden_inputs, memory_blocks=memory_blocks, asking_matrix=asking_matrix, matching_matrix=matching_matrix, content_matrix=content_matrix, projection_back_matrix=projection_back_matrix, word_scale_factor=word_scale_factor, memory_scale_factor=memory_scale_factor, memory_retention_share=memory_retention_share, score_scaling=score_scaling)


def norm_rows(values, gain_row):
    wide = values.astype(jnp.float32)
    meansq = lax.optimization_barrier(jnp.mean(wide * wide, axis=-1, keepdims=True))
    return (wide * lax.rsqrt(meansq + 1e-06) * gain_row).astype(jnp.bfloat16)

def incomplete_heads_sum(rescaled_lines, state_count, proj_query, proj_key, proj_value, proj_out, scratch_numbers):
    row_count = rescaled_lines.shape[0]
    head_count = proj_query.shape[1] // HEAD_DIM
    queries = jnp.dot(rescaled_lines, proj_query, preferred_element_type=jnp.float32).astype(jnp.bfloat16).reshape(row_count, head_count, HEAD_DIM)
    key_rows = jnp.dot(rescaled_lines, proj_key, preferred_element_type=jnp.float32).astype(jnp.bfloat16).reshape(row_count, head_count, HEAD_DIM)
    value_rows = jnp.dot(rescaled_lines, proj_value, preferred_element_type=jnp.float32).astype(jnp.bfloat16).reshape(row_count, head_count, HEAD_DIM)
    scores = jnp.einsum('qhd,khd->hqk', queries.astype(jnp.float32), key_rows.astype(jnp.float32))
    scaled = scores * (scratch_numbers / math.sqrt(HEAD_DIM))[:, None, None]
    query_pos = jnp.arange(row_count, dtype=jnp.int32)[:, None]
    key_pos = jnp.arange(row_count, dtype=jnp.int32)[None, :]
    allowed = (key_pos < state_count) | (query_pos < state_count) | (key_pos <= query_pos)
    masked = jnp.where(allowed[None], scaled, -jnp.inf)
    row_peak = lax.optimization_barrier(jnp.max(masked, axis=-1, keepdims=True))
    exponent = jnp.exp(masked - row_peak)
    weights = (exponent / lax.optimization_barrier(jnp.sum(exponent, axis=-1, keepdims=True))).astype(jnp.bfloat16)
    mixed_heads = jnp.einsum('hqk,khd->qhd', weights.astype(jnp.float32), value_rows.astype(jnp.float32))
    mixed_heads = mixed_heads.astype(jnp.bfloat16).reshape(row_count, head_count * HEAD_DIM)
    return jnp.dot(mixed_heads, proj_out, preferred_element_type=jnp.float32).astype(jnp.bfloat16)

def mesh_place(depth_level, word_lines, carried_memory, asking_matrix, matching_matrix, content_matrix, projection_back_matrix, word_scale_factor, memory_scale_factor, memory_retention_share, score_scaling):
    rescaled_lines = jnp.concatenate([norm_rows(carried_memory, memory_scale_factor[depth_level]), norm_rows(word_lines, word_scale_factor[depth_level])], axis=0)
    total_accumulated = jnp.zeros(rescaled_lines.shape, jnp.float32)
    for pair_half in range(2):
        parameter_offset = 2 * depth_level + pair_half
        total_accumulated = total_accumulated + incomplete_heads_sum(rescaled_lines, MEMORY_LINES, asking_matrix[parameter_offset], matching_matrix[parameter_offset], content_matrix[parameter_offset], projection_back_matrix[parameter_offset], score_scaling[parameter_offset]).astype(jnp.float32)
    token_out = (word_lines.astype(jnp.float32) + total_accumulated[MEMORY_LINES:]).astype(jnp.bfloat16)
    retain = memory_retention_share[depth_level]
    state_out = (retain * carried_memory.astype(jnp.float32) + (1.0 - retain) * total_accumulated[:MEMORY_LINES]).astype(jnp.bfloat16)
    return (token_out, state_out)

def reference(passage_word_codes, word_vector_lookup, hidden_inputs, memory_blocks, asking_matrix, matching_matrix, content_matrix, projection_back_matrix, word_scale_factor, memory_scale_factor, memory_retention_share, score_scaling):

    def run_step(tok_all, st_all):

        def one_cell(item):
            entry_offset, word_lines, carried_memory = item
            return mesh_place(entry_offset % DEPTH_TOTAL, word_lines, carried_memory, asking_matrix, matching_matrix, content_matrix, projection_back_matrix, word_scale_factor, memory_scale_factor, memory_retention_share, score_scaling)
        return lax.map(one_cell, (jnp.arange(N_SEG * DEPTH_TOTAL, dtype=jnp.int32), tok_all, st_all))
    tok_first = hidden_inputs.reshape(N_SEG * DEPTH_TOTAL, SEG_TOK, D)
    st_first = memory_blocks.reshape(N_SEG * DEPTH_TOTAL, MEMORY_LINES, D)
    out_first, new_first = run_step(tok_first, st_first)
    out_grid = out_first.reshape(N_SEG, DEPTH_TOTAL, SEG_TOK, D)
    new_grid = new_first.reshape(N_SEG, DEPTH_TOTAL, MEMORY_LINES, D)
    embedded = jnp.take(word_vector_lookup, passage_word_codes, axis=0)
    tok_second = jnp.concatenate([embedded[:, None], out_grid[:, :-1]], axis=1).reshape(N_SEG * DEPTH_TOTAL, SEG_TOK, D)
    st_second = jnp.roll(new_grid, 1, axis=0).reshape(N_SEG * DEPTH_TOTAL, MEMORY_LINES, D)
    out_second, new_second = run_step(tok_second, st_second)
    return (out_second.reshape(N_SEG, DEPTH_TOTAL * SEG_TOK, D), new_second.reshape(N_SEG, DEPTH_TOTAL * MEMORY_LINES, D))
```

```python
import functools
import math

import jax
import jax.numpy as jnp
from jax import lax
from jax.experimental import pallas as pl
from jax.experimental.pallas import tpu as pltpu
from jax.sharding import PartitionSpec as P

HEAD_DIM = 128
LOG2E = math.log2(math.e)
F32 = jnp.float32
BF16 = jnp.bfloat16
MESH = pl.DeviceIdType.MESH


def cell_kernel(
    n_layers,
    n_seg,
    codes_hbm,
    table_hbm,
    tok_hbm,
    st_hbm,
    wq_hbm,
    wk_hbm,
    wv_hbm,
    wo_hbm,
    wgain_hbm,
    mgain_hbm,
    keep_hbm,
    scale_ref,
    tok_out,
    st_out,
    codes,
    table,
    x1,
    c1,
    wq,
    wk,
    wv,
    wo,
    wgain,
    mgain,
    keep,
    onehot,
    emb_own,
    emb_send,
    emb_got,
    a2a,
    emb_red,
    u1,
    u2,
    q,
    k,
    v,
    o1,
    o2,
    ost,
    x2,
    c2,
    y1,
    s2,
    part_send1,
    part_got1,
    part_send2,
    part_got2,
    part_send3,
    part_got3,
    part_send4,
    part_got4,
    fin_tok,
    fin_st,
    load_sem,
    pair_send,
    pair_recv,
    a2a_send,
    a2a_recv,
    red_send,
    red_recv,
    seg_send,
    seg_recv,
    tok_send,
    tok_recv,
    out_sem,
):
    pos = lax.axis_index("section")
    seg = lax.axis_index("seg")
    layer = pos // 2
    half = pos % 2
    mate = layer * 2 + (1 - half)
    seg_next = lax.rem(seg + 1, n_seg)
    seg_prev = lax.rem(seg + n_seg - 1, n_seg)
    rows = x1.shape[0]
    width = x1.shape[1]
    chunk = width // n_layers
    heads = wq.shape[1] // HEAD_DIM

    barrier = pltpu.get_barrier_semaphore()
    pl.semaphore_signal(barrier, inc=1, device_id={"section": mate}, device_id_type=MESH)
    for other in (seg_next, seg_prev):
        pl.semaphore_signal(barrier, inc=1, device_id={"seg": other}, device_id_type=MESH)

    @pl.loop(1, n_layers)
    def _(step):
        peer = lax.rem(layer + step, n_layers) * 2 + half
        pl.semaphore_signal(barrier, inc=1, device_id={"section": peer}, device_id_type=MESH)

    pairs = (
        (st_hbm, c1),
        (tok_hbm, x1),
        (mgain_hbm, mgain),
        (wgain_hbm, wgain),
        (codes_hbm, codes),
        (table_hbm, table),
        (wq_hbm, wq),
        (wk_hbm, wk),
        (wv_hbm, wv),
        (keep_hbm, keep),
        (wo_hbm, wo),
    )
    loads = [pltpu.make_async_copy(a, b, load_sem.at[i]) for i, (a, b) in enumerate(pairs)]
    for load in loads:
        load.start()

    def norm_into(src, gain_ref, dst, base):
        gain = gain_ref[pl.ds(layer, 1), :]

        @pl.loop(0, rows // 16)
        def _(i):
            r = pl.multiple_of(i * 16, 16)
            wide = src[pl.ds(r, 16), :].astype(F32)
            meansq = jnp.mean(wide * wide, axis=-1, keepdims=True)
            dst[pl.ds(base + r, 16), :] = (wide * lax.rsqrt(meansq + 1e-06) * gain).astype(BF16)

    def to_mate(src, dst, i):
        return pltpu.make_async_remote_copy(
            src_ref=src,
            dst_ref=dst,
            send_sem=pair_send.at[i],
            recv_sem=pair_recv.at[i],
            device_id={"section": mate},
            device_id_type=MESH,
        )

    def to_seg(src, dst, i):
        return pltpu.make_async_remote_copy(
            src_ref=src,
            dst_ref=dst,
            send_sem=seg_send.at[i],
            recv_sem=seg_recv.at[i],
            device_id={"seg": seg_next},
            device_id_type=MESH,
        )

    def project(u, base):
        block = u[pl.ds(base, 2 * rows), :]
        for w, dst in ((wq, q), (wk, k), (wv, v)):
            dst[pl.ds(base, 2 * rows), :] = jnp.dot(
                block, w[...], preferred_element_type=F32
            ).astype(BF16)

    def attend(o, first, masked):
        @pl.loop(0, 2)
        def _(b):
            base = pl.multiple_of(first + b * rows, rows)
            if masked:
                col = lax.broadcasted_iota(jnp.int32, (rows, 4 * rows), 1)
                row = lax.broadcasted_iota(jnp.int32, (rows, 4 * rows), 0)
                own = half * rows
                far = (1 - half) * rows
                kpos = jnp.where(
                    col < 2 * rows,
                    -1,
                    jnp.where(col < 3 * rows, col - 2 * rows + own, col - 3 * rows + far),
                )
                qpos = row + (own + b * (far - own))
                allowed = kpos <= qpos
            for h in range(heads):
                lanes = pl.ds(h * HEAD_DIM, HEAD_DIM)
                s = lax.dot_general(
                    q[pl.ds(base, rows), lanes],
                    k[:, lanes],
                    (((1,), (1,)), ((), ())),
                    preferred_element_type=F32,
                )
                s = s * (scale_ref[0, h] * (LOG2E / math.sqrt(HEAD_DIM)))
                if masked:
                    s = jnp.where(allowed, s, -jnp.inf)
                e = jnp.exp2(s - jnp.max(s, axis=-1, keepdims=True))
                p = (e * (1.0 / jnp.sum(e, axis=-1, keepdims=True))).astype(BF16)
                o[pl.ds(base, rows), lanes] = jnp.dot(
                    p, v[:, lanes], preferred_element_type=F32
                ).astype(BF16)

    def back(o, base, dst):
        dst[...] = jnp.dot(
            o[pl.ds(base, rows), :], wo[...], preferred_element_type=F32
        ).astype(BF16)

    def token_sum(o, base, x, got, dst):
        @pl.loop(0, width // 512)
        def _(t):
            cols = pl.ds(pl.multiple_of(t * 512, 512), 512)
            mine = jnp.dot(
                o[pl.ds(base, rows), :], wo[:, cols], preferred_element_type=F32
            ).astype(BF16)
            total = mine.astype(F32) + got[:, cols].astype(F32)
            dst[:, cols] = (x[:, cols].astype(F32) + total).astype(BF16)

    def state_sum(o, base, c, got, dst):
        @pl.loop(0, width // 512)
        def _(t):
            cols = pl.ds(pl.multiple_of(t * 512, 512), 512)
            mine = jnp.dot(
                o[pl.ds(base, rows), :], wo[:, cols], preferred_element_type=F32
            ).astype(BF16)
            total = mine.astype(F32) + got[:, cols].astype(F32)
            r = keep[pl.ds(layer, 1), cols]
            dst[:, cols] = (r * c[:, cols].astype(F32) + (1.0 - r) * total).astype(BF16)

    loads[0].wait()
    loads[2].wait()
    norm_into(c1, mgain, u1, 0)
    loads[1].wait()
    loads[3].wait()
    norm_into(x1, wgain, u1, 2 * rows)
    pl.semaphore_wait(barrier, n_layers + 2)
    send_u1s = to_mate(u1.at[pl.ds(0, rows)], u1.at[pl.ds(rows, rows)], 0)
    send_u1s.start()
    send_u1t = to_mate(u1.at[pl.ds(2 * rows, rows)], u1.at[pl.ds(3 * rows, rows)], 1)
    send_u1t.start()
    send_c = to_seg(c1, c2, 0)
    send_c.start()

    loads[4].wait()
    vocab = table.shape[0]
    ids = jnp.broadcast_to(codes[...].astype(F32), (HEAD_DIM, 2 * rows)).T
    lane = lax.broadcasted_iota(jnp.int32, ids.shape, 1) + pos * vocab
    for b in range(vocab // HEAD_DIM):
        hit = ids == (lane + b * HEAD_DIM).astype(F32)
        onehot[:, b * HEAD_DIM : (b + 1) * HEAD_DIM] = jnp.where(hit, 1.0, 0.0).astype(BF16)
    loads[5].wait()
    own_rows = pl.ds(pl.multiple_of(half * rows, rows), rows)
    far_rows = pl.ds(pl.multiple_of((1 - half) * rows, rows), rows)

    @pl.loop(0, n_layers)
    def _(j):
        cols = pl.ds(pl.multiple_of(j * chunk, chunk), chunk)
        part = table[:, cols]
        emb_send[j] = jnp.dot(onehot[far_rows, :], part, preferred_element_type=F32).astype(BF16)
        emb_own[j] = jnp.dot(onehot[own_rows, :], part, preferred_element_type=F32).astype(BF16)

    send_emb = to_mate(emb_send, emb_got, 2)
    send_emb.start()

    send_u1s.wait_recv()
    loads[6].wait()
    loads[7].wait()
    loads[8].wait()
    project(u1, 0)

    send_emb.wait_recv()
    emb_own[...] = emb_own[...] + emb_got[...]

    def a2a_copy(step):
        peer = lax.rem(layer + step, n_layers)
        return pltpu.make_async_remote_copy(
            src_ref=emb_own.at[peer],
            dst_ref=a2a.at[layer],
            send_sem=a2a_send.at[peer],
            recv_sem=a2a_recv.at[layer],
            device_id={"section": peer * 2 + half},
            device_id_type=MESH,
        )

    def a2a_arrival(step):
        peer = lax.rem(layer + step, n_layers)
        return pltpu.make_async_remote_copy(
            src_ref=emb_own.at[layer],
            dst_ref=a2a.at[peer],
            send_sem=a2a_send.at[layer],
            recv_sem=a2a_recv.at[peer],
            device_id={"section": peer * 2 + half},
            device_id_type=MESH,
        )

    @pl.loop(1, n_layers)
    def _(step):
        a2a_copy(step).start()

    send_u1t.wait_recv()
    project(u1, 2 * rows)

    attend(o1, 2 * rows, True)
    loads[10].wait()
    back(o1, 3 * rows, part_send1)
    send_p1 = to_mate(part_send1, part_got1, 3)
    send_p1.start()
    send_p1.wait_recv()
    token_sum(o1, 2 * rows, x1, part_got1, y1)

    def token_copy(target):
        return pltpu.make_async_remote_copy(
            src_ref=y1,
            dst_ref=x2,
            send_sem=tok_send,
            recv_sem=tok_recv,
            device_id={"section": target},
            device_id_type=MESH,
        )

    last = n_layers - 1
    up = jnp.where(layer < last, pos + 2, pos - 2 * last)

    @pl.when(layer < last)
    def _():
        token_copy(up).start()

    attend(o1, 0, False)
    send_o = to_seg(o1.at[pl.ds(0, 2 * rows)], ost, 1)
    send_o.start()

    emb_red[...] = emb_own[layer]

    @pl.loop(1, n_layers)
    def _(step):
        a2a_arrival(step).wait_recv()
        emb_red[...] = emb_red[...] + a2a[lax.rem(layer + step, n_layers)]

    my_cols = pl.ds(pl.multiple_of(layer * chunk, chunk), chunk)

    def red_copy():
        return pltpu.make_async_remote_copy(
            src_ref=emb_red,
            dst_ref=x2.at[:, my_cols],
            send_sem=red_send,
            recv_sem=red_recv.at[layer],
            device_id={"section": half},
            device_id_type=MESH,
        )

    @pl.when(layer > 0)
    def _():
        red_copy().start()

    send_o.wait_recv()
    back(ost, rows, part_send2)
    send_p2 = to_mate(part_send2, part_got2, 4)
    send_p2.start()
    send_c.wait_recv()
    loads[9].wait()
    send_p2.wait_recv()
    state_sum(ost, 0, c2, part_got2, s2)
    norm_into(s2, mgain, u2, 0)
    send_u2s = to_mate(u2.at[pl.ds(0, rows)], u2.at[pl.ds(rows, rows)], 5)
    send_u2s.start()
    send_u2s.wait_recv()
    project(u2, 0)

    @pl.when(layer > 0)
    def _():
        token_copy(up).wait_recv()

    @pl.when(layer == 0)
    def _():
        x2[:, 0:chunk] = emb_red[...]

        @pl.loop(1, n_layers)
        def _(i):
            cols = pl.ds(pl.multiple_of(i * chunk, chunk), chunk)
            pltpu.make_async_remote_copy(
                src_ref=emb_red,
                dst_ref=x2.at[:, cols],
                send_sem=red_send,
                recv_sem=red_recv.at[i],
                device_id={"section": mate},
                device_id_type=MESH,
            ).wait_recv()

    norm_into(x2, wgain, u2, 2 * rows)
    send_u2t = to_mate(u2.at[pl.ds(2 * rows, rows)], u2.at[pl.ds(3 * rows, rows)], 6)
    send_u2t.start()
    send_u2t.wait_recv()
    project(u2, 2 * rows)

    attend(o2, 2 * rows, True)
    back(o2, 3 * rows, part_send3)
    send_p3 = to_mate(part_send3, part_got3, 7)
    send_p3.start()
    attend(o2, 0, False)
    back(o2, rows, part_send4)
    send_p4 = to_mate(part_send4, part_got4, 8)
    send_p4.start()
    send_p3.wait_recv()
    token_sum(o2, 2 * rows, x2, part_got3, fin_tok)
    write_tok = pltpu.make_async_copy(fin_tok, tok_out, out_sem.at[0])
    write_tok.start()
    send_p4.wait_recv()
    state_sum(o2, 0, s2, part_got4, fin_st)
    write_st = pltpu.make_async_copy(fin_st, st_out, out_sem.at[1])
    write_st.start()

    for copy in (
        send_u1s,
        send_u1t,
        send_c,
        send_emb,
        send_p1,
        send_o,
        send_p2,
        send_u2s,
        send_u2t,
        send_p3,
        send_p4,
    ):
        copy.wait_send()

    @pl.loop(1, n_layers)
    def _(step):
        a2a_copy(step).wait_send()

    @pl.when(layer < last)
    def _():
        token_copy(up).wait_send()

    @pl.when(layer > 0)
    def _():
        red_copy().wait_send()

    write_tok.wait()
    write_st.wait()


def per_device(n_layers, n_seg, codes, table, tok, st, wq, wk, wv, wo, wgain, mgain, keep, scale):
    rows, width = tok.shape[1:]
    inner = wq.shape[2]
    vocab = table.shape[0]
    chunk = width // n_layers
    any_spec = pl.BlockSpec(memory_space=pl.ANY)
    act = pltpu.VMEM((rows, width), BF16)
    big = pltpu.VMEM((4 * rows, width), BF16)
    mid = pltpu.VMEM((4 * rows, inner), BF16)
    emb = pltpu.VMEM((n_layers, rows, chunk), BF16)
    gain = pltpu.VMEM(wgain.shape, F32)
    sem = pltpu.SemaphoreType.DMA
    tok_new, st_new = pl.pallas_call(
        functools.partial(cell_kernel, n_layers, n_seg),
        out_shape=(jax.ShapeDtypeStruct((rows, width), BF16),) * 2,
        in_specs=[any_spec] * 11 + [pl.BlockSpec(memory_space=pltpu.SMEM)],
        out_specs=(any_spec, any_spec),
        scratch_shapes=[
            pltpu.VMEM(codes.shape, jnp.int32),
            pltpu.VMEM((vocab, width), BF16),
            act,
            act,
            pltpu.VMEM((width, inner), BF16),
            pltpu.VMEM((width, inner), BF16),
            pltpu.VMEM((width, inner), BF16),
            pltpu.VMEM((inner, width), BF16),
            gain,
            gain,
            gain,
            pltpu.VMEM((codes.shape[1], vocab), BF16),
            emb,
            emb,
            emb,
            emb,
            pltpu.VMEM((rows, chunk), BF16),
            big,
            big,
            mid,
            mid,
            mid,
            mid,
            mid,
            pltpu.VMEM((2 * rows, inner), BF16),
        ]
        + [act] * 14
        + [
            sem((11,)),
            sem((9,)),
            sem((9,)),
            sem((n_layers,)),
            sem((n_layers,)),
            sem,
            sem((n_layers,)),
            sem((2,)),
            sem((2,)),
            sem,
            sem,
            sem((2,)),
        ],
        compiler_params=pltpu.CompilerParams(
            collective_id=0, has_side_effects=True, vmem_limit_bytes=58 * 1024 * 1024
        ),
    )(
        codes,
        table,
        tok[0],
        st[0],
        wq[0],
        wk[0],
        wv[0],
        wo[0],
        wgain,
        mgain,
        keep,
        scale,
    )
    return (tok_new[None], st_new[None])


def solution(mesh):
    placed = (
        P("seg", None),
        P("section", None),
        P("seg", "section", None),
        P("seg", "section", None),
        P("section", None, None),
        P("section", None, None),
        P("section", None, None),
        P("section", None, None),
        P(),
        P(),
        P(),
        P("section", None),
    )
    return jax.shard_map(
        functools.partial(per_device, mesh.shape["section"] // 2, mesh.shape["seg"]),
        mesh=mesh,
        in_specs=placed,
        out_specs=(P("seg", "section", None), P("seg", "section", None)),
        check_vma=False,
    )
```

```python
import functools
import math

import jax
import jax.numpy as jnp
from jax import lax
from jax.experimental import pallas as pl
from jax.experimental.pallas import tpu as pltpu
from jax.sharding import PartitionSpec as P

HEAD_DIM = 128
LOG2E = math.log2(math.e)
F32 = jnp.float32
BF16 = jnp.bfloat16
MESH = pl.DeviceIdType.MESH


def cell_kernel(
    n_layers,
    n_seg,
    codes_hbm,
    table_hbm,
    tok_hbm,
    st_hbm,
    wq_hbm,
    wk_hbm,
    wv_hbm,
    wo_hbm,
    wgain_hbm,
    mgain_hbm,
    keep_hbm,
    scale_ref,
    tok_out,
    st_out,
    codes,
    table,
    x1,
    c1,
    wq,
    wk,
    wv,
    wo,
    wgain,
    mgain,
    keep,
    onehot,
    emb_own,
    emb_send,
    emb_got,
    a2a,
    emb_red,
    u1,
    u2,
    q,
    k,
    v,
    o1,
    o2,
    ost,
    x2,
    c2,
    y1,
    s2,
    send_a,
    got_a,
    send_b,
    got_b,
    send_c_part,
    got_c_part,
    send_d,
    got_d,
    fin_tok,
    fin_st,
    kept_a,
    kept_b,
    kept_c,
    kept_d,
    load_sem,
    pair_send,
    pair_recv,
    part_ssem,
    part_rsem,
    a2a_send,
    a2a_recv,
    red_send,
    red_recv,
    seg_send,
    seg_recv,
    tok_send,
    tok_recv,
    out_sem,
):
    pos = lax.axis_index("section")
    seg = lax.axis_index("seg")
    layer = pos // 2
    half = pos % 2
    mate = layer * 2 + (1 - half)
    seg_next = lax.rem(seg + 1, n_seg)
    seg_prev = lax.rem(seg + n_seg - 1, n_seg)
    rows = x1.shape[0]
    width = x1.shape[1]
    chunk = width // n_layers
    heads = wq.shape[1] // HEAD_DIM
    kept = (kept_a, kept_b, kept_c, kept_d)
    parts = ((send_a, got_a), (send_b, got_b), (send_c_part, got_c_part), (send_d, got_d))

    barrier = pltpu.get_barrier_semaphore()
    pl.semaphore_signal(barrier, inc=1, device_id={"section": mate}, device_id_type=MESH)
    for other in (seg_next, seg_prev):
        pl.semaphore_signal(barrier, inc=1, device_id={"seg": other}, device_id_type=MESH)

    @pl.loop(1, n_layers)
    def _(step):
        peer = lax.rem(layer + step, n_layers) * 2 + half
        pl.semaphore_signal(barrier, inc=1, device_id={"section": peer}, device_id_type=MESH)

    pairs = (
        (st_hbm, c1),
        (tok_hbm, x1),
        (mgain_hbm, mgain),
        (wgain_hbm, wgain),
        (codes_hbm, codes),
        (table_hbm, table),
        (wq_hbm, wq),
        (wk_hbm, wk),
        (wv_hbm, wv),
        (keep_hbm, keep),
        (wo_hbm, wo),
    )
    loads = [pltpu.make_async_copy(a, b, load_sem.at[i]) for i, (a, b) in enumerate(pairs)]
    for load in loads[:6]:
        load.start()

    def norm_into(src, gain_ref, dst, base, first=0, count=rows):
        gain = gain_ref[pl.ds(layer, 1), :]

        @pl.loop(0, count // 16)
        def _(i):
            r = pl.multiple_of(first + i * 16, 16)
            wide = src[pl.ds(r, 16), :].astype(F32)
            meansq = jnp.mean(wide * wide, axis=-1, keepdims=True)
            dst[pl.ds(base + r, 16), :] = (wide * lax.rsqrt(meansq + 1e-06) * gain).astype(BF16)

    def to_mate(src, dst, i):
        return pltpu.make_async_remote_copy(
            src_ref=src,
            dst_ref=dst,
            send_sem=pair_send.at[i],
            recv_sem=pair_recv.at[i],
            device_id={"section": mate},
            device_id_type=MESH,
        )

    def to_seg(src, dst, i):
        return pltpu.make_async_remote_copy(
            src_ref=src,
            dst_ref=dst,
            send_sem=seg_send.at[i],
            recv_sem=seg_recv.at[i],
            device_id={"seg": seg_next},
            device_id_type=MESH,
        )

    def project(u, base):
        block = u[pl.ds(base, 2 * rows), :]
        for w, dst in ((wq, q), (wk, k), (wv, v)):
            dst[pl.ds(base, 2 * rows), :] = jnp.dot(
                block, w[...], preferred_element_type=F32
            ).astype(BF16)

    def attend(o, first, masked, some=tuple(range(heads))):
        block = pl.ds(first, 2 * rows)
        if masked:
            col = lax.broadcasted_iota(jnp.int32, (1, 4 * rows), 1)
            row = lax.broadcasted_iota(jnp.int32, (2 * rows, 1), 0)
            own = half * rows
            far = (1 - half) * rows
            kpos = jnp.where(
                col < 2 * rows,
                -1,
                jnp.where(col < 3 * rows, col - 2 * rows + own, col - 3 * rows + far),
            )
            qpos = jnp.where(row < rows, row + own, row - rows + far)
        for h in some:
            lanes = pl.ds(h * HEAD_DIM, HEAD_DIM)
            s = lax.dot_general(
                q[block, lanes],
                k[:, lanes],
                (((1,), (1,)), ((), ())),
                preferred_element_type=F32,
            )
            s = s * (scale_ref[0, h] * (LOG2E / math.sqrt(HEAD_DIM)))
            if masked:
                s = jnp.where(kpos <= qpos, s, -jnp.inf)
            e = jnp.exp2(s - jnp.max(s, axis=-1, keepdims=True))
            p = (e * (1.0 / jnp.sum(e, axis=-1, keepdims=True))).astype(BF16)
            o[block, lanes] = jnp.dot(p, v[:, lanes], preferred_element_type=F32).astype(BF16)

    tiles = 4
    span = width // tiles

    def part_copy(which, t):
        send, got = parts[which]
        cols = pl.ds(pl.multiple_of(t * span, span), span)
        return pltpu.make_async_remote_copy(
            src_ref=send.at[:, cols],
            dst_ref=got.at[:, cols],
            send_sem=part_ssem.at[which * tiles + t],
            recv_sem=part_rsem.at[which * tiles + t],
            device_id={"section": mate},
            device_id_type=MESH,
        )

    def back(o, base, which):
        @pl.loop(0, tiles)
        def _(t):
            cols = pl.ds(pl.multiple_of(t * span, span), span)
            both = jnp.dot(
                o[pl.ds(base, 2 * rows), :], wo[:, cols], preferred_element_type=F32
            ).astype(BF16)
            parts[which][0][:, cols] = both[rows:]
            kept[which][:, cols] = both[:rows]
            part_copy(which, t).start()

    def summed(which, finish, after=None):
        @pl.loop(0, tiles)
        def _(t):
            cols = pl.ds(pl.multiple_of(t * span, span), span)
            part_copy(which, t).wait_recv()
            finish(cols, kept[which][:, cols].astype(F32) + parts[which][1][:, cols].astype(F32))
            if after is not None:
                after(t)

    def token_finish(x, dst):
        def finish(cols, total):
            dst[:, cols] = (x[:, cols].astype(F32) + total).astype(BF16)

        return finish

    def state_finish(c, dst):
        def finish(cols, total):
            r = keep[pl.ds(layer, 1), cols]
            dst[:, cols] = (r * c[:, cols].astype(F32) + (1.0 - r) * total).astype(BF16)

        return finish

    loads[0].wait()
    loads[2].wait()
    loads[1].wait()
    loads[3].wait()
    for load in loads[6:]:
        load.start()
    norm_into(c1, mgain, u1, 0)
    norm_into(x1, wgain, u1, 2 * rows)
    pl.semaphore_wait(barrier, n_layers + 2)
    send_u1s = to_mate(u1.at[pl.ds(0, rows)], u1.at[pl.ds(rows, rows)], 0)
    send_u1s.start()
    send_u1t = to_mate(u1.at[pl.ds(2 * rows, rows)], u1.at[pl.ds(3 * rows, rows)], 1)
    send_u1t.start()
    send_c = to_seg(c1, c2, 0)
    send_c.start()

    loads[4].wait()
    vocab = table.shape[0]
    ids = jnp.broadcast_to(codes[...].astype(F32), (HEAD_DIM, 2 * rows)).T
    lane = lax.broadcasted_iota(jnp.int32, ids.shape, 1) + pos * vocab
    for b in range(vocab // HEAD_DIM):
        hit = ids == (lane + b * HEAD_DIM).astype(F32)
        onehot[:, b * HEAD_DIM : (b + 1) * HEAD_DIM] = jnp.where(hit, 1.0, 0.0).astype(BF16)
    loads[5].wait()
    own_rows = pl.ds(pl.multiple_of(half * rows, rows), rows)
    far_rows = pl.ds(pl.multiple_of((1 - half) * rows, rows), rows)

    @pl.loop(0, n_layers)
    def _(j):
        cols = pl.ds(pl.multiple_of(j * chunk, chunk), chunk)
        part = table[:, cols]
        emb_send[j] = jnp.dot(onehot[far_rows, :], part, preferred_element_type=F32).astype(BF16)
        emb_own[j] = jnp.dot(onehot[own_rows, :], part, preferred_element_type=F32).astype(BF16)

    send_emb = to_mate(emb_send, emb_got, 2)
    send_emb.start()

    send_u1s.wait_recv()
    loads[6].wait()
    loads[7].wait()
    loads[8].wait()
    project(u1, 0)

    send_emb.wait_recv()
    emb_own[...] = emb_own[...] + emb_got[...]

    def a2a_copy(step):
        peer = lax.rem(layer + step, n_layers)
        return pltpu.make_async_remote_copy(
            src_ref=emb_own.at[peer],
            dst_ref=a2a.at[layer],
            send_sem=a2a_send.at[peer],
            recv_sem=a2a_recv.at[layer],
            device_id={"section": peer * 2 + half},
            device_id_type=MESH,
        )

    def a2a_arrival(step):
        peer = lax.rem(layer + step, n_layers)
        return pltpu.make_async_remote_copy(
            src_ref=emb_own.at[layer],
            dst_ref=a2a.at[peer],
            send_sem=a2a_send.at[layer],
            recv_sem=a2a_recv.at[peer],
            device_id={"section": peer * 2 + half},
            device_id_type=MESH,
        )

    @pl.loop(1, n_layers)
    def _(step):
        a2a_copy(step).start()

    send_u1t.wait_recv()
    project(u1, 2 * rows)

    attend(o1, 2 * rows, True)
    loads[10].wait()
    back(o1, 2 * rows, 0)

    last = n_layers - 1
    up = jnp.where(layer < last, pos + 2, pos - 2 * last)
    upper = rows // 2

    def token_copy(row, cols, i):
        return pltpu.make_async_remote_copy(
            src_ref=y1.at[pl.ds(row, upper), cols],
            dst_ref=x2.at[pl.ds(row, upper), cols],
            send_sem=tok_send.at[i],
            recv_sem=tok_recv.at[i],
            device_id={"section": up},
            device_id_type=MESH,
        )

    def upper_copy(t):
        return token_copy(0, pl.ds(pl.multiple_of(t * span, span), span), t)

    def lower_copy():
        return token_copy(upper, pl.ds(0, width), tiles)

    def send_tile(t):
        @pl.when(layer < last)
        def _():
            upper_copy(t).start()

    def send_heads(i):
        lanes = pl.ds(i * (heads // 2) * HEAD_DIM, (heads // 2) * HEAD_DIM)
        copy = to_seg(o1.at[pl.ds(0, 2 * rows), lanes], ost.at[:, lanes], 1 + i)
        copy.start()
        return copy

    attend(o1, 0, False, range(heads // 2))
    send_o0 = send_heads(0)
    summed(0, token_finish(x1, y1), send_tile)

    @pl.when(layer < last)
    def _():
        lower_copy().start()

    attend(o1, 0, False, range(heads // 2, heads))
    send_o1 = send_heads(1)

    emb_red[...] = emb_own[layer]

    @pl.loop(1, n_layers)
    def _(step):
        a2a_arrival(step).wait_recv()
        emb_red[...] = emb_red[...] + a2a[lax.rem(layer + step, n_layers)]

    my_cols = pl.ds(pl.multiple_of(layer * chunk, chunk), chunk)

    def red_copy():
        return pltpu.make_async_remote_copy(
            src_ref=emb_red,
            dst_ref=x2.at[:, my_cols],
            send_sem=red_send,
            recv_sem=red_recv.at[layer],
            device_id={"section": half},
            device_id_type=MESH,
        )

    @pl.when(layer > 0)
    def _():
        red_copy().start()

    send_o0.wait_recv()
    send_o1.wait_recv()
    back(ost, 0, 1)
    send_c.wait_recv()
    loads[9].wait()
    summed(1, state_finish(c2, s2))
    norm_into(s2, mgain, u2, 0)
    send_u2s = to_mate(u2.at[pl.ds(0, rows)], u2.at[pl.ds(rows, rows)], 3)
    send_u2s.start()
    send_u2s.wait_recv()
    project(u2, 0)

    @pl.when(layer > 0)
    def _():
        @pl.loop(0, tiles)
        def _(t):
            upper_copy(t).wait_recv()

    @pl.when(layer == 0)
    def _():
        x2[:, 0:chunk] = emb_red[...]

        @pl.loop(1, n_layers)
        def _(i):
            cols = pl.ds(pl.multiple_of(i * chunk, chunk), chunk)
            pltpu.make_async_remote_copy(
                src_ref=emb_red,
                dst_ref=x2.at[:, cols],
                send_sem=red_send,
                recv_sem=red_recv.at[i],
                device_id={"section": mate},
                device_id_type=MESH,
            ).wait_recv()

    norm_into(x2, wgain, u2, 2 * rows, 0, upper)
    send_u2a = to_mate(u2.at[pl.ds(2 * rows, upper)], u2.at[pl.ds(3 * rows, upper)], 4)
    send_u2a.start()

    @pl.when(layer > 0)
    def _():
        lower_copy().wait_recv()

    norm_into(x2, wgain, u2, 2 * rows, upper, upper)
    send_u2b = to_mate(
        u2.at[pl.ds(2 * rows + upper, upper)], u2.at[pl.ds(3 * rows + upper, upper)], 5
    )
    send_u2b.start()
    send_u2a.wait_recv()
    send_u2b.wait_recv()
    project(u2, 2 * rows)

    attend(o2, 2 * rows, True)
    back(o2, 2 * rows, 2)
    attend(o2, 0, False)
    back(o2, 0, 3)
    summed(2, token_finish(x2, fin_tok))
    write_tok = pltpu.make_async_copy(fin_tok, tok_out, out_sem.at[0])
    write_tok.start()
    summed(3, state_finish(s2, fin_st))
    write_st = pltpu.make_async_copy(fin_st, st_out, out_sem.at[1])
    write_st.start()

    for copy in (
        send_u1s,
        send_u1t,
        send_c,
        send_emb,
        send_o0,
        send_o1,
        send_u2s,
        send_u2a,
        send_u2b,
    ):
        copy.wait_send()

    @pl.loop(1, n_layers)
    def _(step):
        a2a_copy(step).wait_send()

    for which in range(len(parts)):

        @pl.loop(0, tiles)
        def _(t, which=which):
            part_copy(which, t).wait_send()

    @pl.when(layer < last)
    def _():
        @pl.loop(0, tiles)
        def _(t):
            upper_copy(t).wait_send()

        lower_copy().wait_send()

    @pl.when(layer > 0)
    def _():
        red_copy().wait_send()

    write_tok.wait()
    write_st.wait()


def write_kernel(tok_in, st_in, tok_out, st_out, sems):
    copies = (
        pltpu.make_async_copy(tok_in, tok_out, sems.at[0]),
        pltpu.make_async_copy(st_in, st_out, sems.at[1]),
    )
    for copy in copies:
        copy.start()
    for copy in copies:
        copy.wait()


def per_device(n_layers, n_seg, codes, table, tok, st, wq, wk, wv, wo, wgain, mgain, keep, scale):
    rows, width = tok.shape[1:]
    inner = wq.shape[2]
    vocab = table.shape[0]
    chunk = width // n_layers
    any_spec = pl.BlockSpec(memory_space=pl.ANY)
    act = pltpu.VMEM((rows, width), BF16)
    big = pltpu.VMEM((4 * rows, width), BF16)
    mid = pltpu.VMEM((4 * rows, inner), BF16)
    emb = pltpu.VMEM((n_layers, rows, chunk), BF16)
    gain = pltpu.VMEM(wgain.shape, F32)
    sem = pltpu.SemaphoreType.DMA
    tok_new, st_new = pl.pallas_call(
        functools.partial(cell_kernel, n_layers, n_seg),
        out_shape=(jax.ShapeDtypeStruct((rows, width), BF16),) * 2,
        in_specs=[any_spec] * 11 + [pl.BlockSpec(memory_space=pltpu.SMEM)],
        out_specs=(any_spec, any_spec),
        scratch_shapes=[
            pltpu.VMEM(codes.shape, jnp.int32),
            pltpu.VMEM((vocab, width), BF16),
            act,
            act,
            pltpu.VMEM((width, inner), BF16),
            pltpu.VMEM((width, inner), BF16),
            pltpu.VMEM((width, inner), BF16),
            pltpu.VMEM((inner, width), BF16),
            gain,
            gain,
            gain,
            pltpu.VMEM((codes.shape[1], vocab), BF16),
            emb,
            emb,
            emb,
            emb,
            pltpu.VMEM((rows, chunk), BF16),
            big,
            big,
            mid,
            mid,
            mid,
            mid,
            mid,
            pltpu.VMEM((2 * rows, inner), BF16),
        ]
        + [act] * 18
        + [
            sem((11,)),
            sem((6,)),
            sem((6,)),
            sem((16,)),
            sem((16,)),
            sem((n_layers,)),
            sem((n_layers,)),
            sem,
            sem((n_layers,)),
            sem((3,)),
            sem((3,)),
            sem((5,)),
            sem((5,)),
            sem((2,)),
        ],
        compiler_params=pltpu.CompilerParams(
            collective_id=0, has_side_effects=True, vmem_limit_bytes=58 * 1024 * 1024
        ),
    )(
        codes,
        table,
        tok[0],
        st[0],
        wq[0],
        wk[0],
        wv[0],
        wo[0],
        wgain,
        mgain,
        keep,
        scale,
    )
    tok_new, st_new = pl.pallas_call(
        write_kernel,
        out_shape=(jax.ShapeDtypeStruct((rows, width), BF16),) * 2,
        in_specs=[pl.BlockSpec(memory_space=pltpu.VMEM)] * 2,
        out_specs=(any_spec, any_spec),
        scratch_shapes=[sem((2,))],
    )(tok_new, st_new)
    return (tok_new[None], st_new[None])


def solution(mesh):
    placed = (
        P("seg", None),
        P("section", None),
        P("seg", "section", None),
        P("seg", "section", None),
        P("section", None, None),
        P("section", None, None),
        P("section", None, None),
        P("section", None, None),
        P(),
        P(),
        P(),
        P("section", None),
    )
    return jax.shard_map(
        functools.partial(per_device, mesh.shape["section"] // 2, mesh.shape["seg"]),
        mesh=mesh,
        in_specs=placed,
        out_specs=(P("seg", "section", None), P("seg", "section", None)),
        check_vma=False,
    )
```

```python
import functools
import math

import jax
import jax.numpy as jnp
from jax import lax
from jax.experimental import pallas as pl
from jax.experimental.pallas import tpu as pltpu
from jax.sharding import PartitionSpec as P

HEAD_DIM = 128
LOG2E = math.log2(math.e)
F32 = jnp.float32
BF16 = jnp.bfloat16
MESH = pl.DeviceIdType.MESH


def cell_kernel(
    n_layers,
    n_seg,
    codes_hbm,
    table_hbm,
    tok_hbm,
    st_hbm,
    wq_hbm,
    wk_hbm,
    wv_hbm,
    wo_hbm,
    wgain_hbm,
    mgain_hbm,
    keep_hbm,
    scale_ref,
    tok_out,
    st_out,
    codes,
    table,
    x1,
    c1,
    wq,
    wk,
    wv,
    wo,
    wgain,
    mgain,
    keep,
    onehot,
    emb_own,
    emb_send,
    emb_got,
    a2a,
    emb_red,
    u1,
    u2,
    q,
    k,
    v,
    o1,
    o2,
    ost,
    x2,
    c2,
    y1,
    s2,
    send_a,
    got_a,
    send_b,
    got_b,
    send_c_part,
    got_c_part,
    send_d,
    got_d,
    fin_tok,
    fin_st,
    kept_a,
    kept_b,
    kept_c,
    kept_d,
    load_sem,
    pair_send,
    pair_recv,
    part_ssem,
    part_rsem,
    a2a_send,
    a2a_recv,
    red_send,
    red_recv,
    seg_send,
    seg_recv,
    tok_send,
    tok_recv,
    out_sem,
):
    pos = lax.axis_index("section")
    seg = lax.axis_index("seg")
    layer = pos // 2
    half = pos % 2
    mate = layer * 2 + (1 - half)
    seg_next = lax.rem(seg + 1, n_seg)
    seg_prev = lax.rem(seg + n_seg - 1, n_seg)
    rows = x1.shape[0]
    width = x1.shape[1]
    chunk = width // n_layers
    heads = wq.shape[1] // HEAD_DIM
    kept = (kept_a, kept_b, kept_c, kept_d)
    parts = ((send_a, got_a), (send_b, got_b), (send_c_part, got_c_part), (send_d, got_d))

    barrier = pltpu.get_barrier_semaphore()
    pl.semaphore_signal(barrier, inc=1, device_id={"section": mate}, device_id_type=MESH)
    for other in (seg_next, seg_prev):
        pl.semaphore_signal(barrier, inc=1, device_id={"seg": other}, device_id_type=MESH)

    @pl.loop(1, n_layers)
    def _(step):
        peer = lax.rem(layer + step, n_layers) * 2 + half
        pl.semaphore_signal(barrier, inc=1, device_id={"section": peer}, device_id_type=MESH)

    pairs = (
        (st_hbm, c1),
        (tok_hbm, x1),
        (mgain_hbm, mgain),
        (wgain_hbm, wgain),
        (codes_hbm, codes),
        (table_hbm, table),
        (wq_hbm, wq),
        (wk_hbm, wk),
        (wv_hbm, wv),
        (keep_hbm, keep),
        (wo_hbm, wo),
    )
    loads = [pltpu.make_async_copy(a, b, load_sem.at[i]) for i, (a, b) in enumerate(pairs)]
    for load in loads[:6]:
        load.start()

    def norm_into(src, gain_ref, dst, base, first=0, count=rows):
        gain = gain_ref[pl.ds(layer, 1), :]

        @pl.loop(0, count // 16)
        def _(i):
            r = pl.multiple_of(first + i * 16, 16)
            wide = src[pl.ds(r, 16), :].astype(F32)
            meansq = jnp.mean(wide * wide, axis=-1, keepdims=True)
            dst[pl.ds(base + r, 16), :] = (wide * lax.rsqrt(meansq + 1e-06) * gain).astype(BF16)

    def to_mate(src, dst, i):
        return pltpu.make_async_remote_copy(
            src_ref=src,
            dst_ref=dst,
            send_sem=pair_send.at[i],
            recv_sem=pair_recv.at[i],
            device_id={"section": mate},
            device_id_type=MESH,
        )

    def to_seg(src, dst, i):
        return pltpu.make_async_remote_copy(
            src_ref=src,
            dst_ref=dst,
            send_sem=seg_send.at[i],
            recv_sem=seg_recv.at[i],
            device_id={"seg": seg_next},
            device_id_type=MESH,
        )

    def project(u, base):
        block = u[pl.ds(base, 2 * rows), :]
        for w, dst in ((wq, q), (wk, k), (wv, v)):
            dst[pl.ds(base, 2 * rows), :] = jnp.dot(
                block, w[...], preferred_element_type=F32
            ).astype(BF16)

    def attend(o, first, masked, some=tuple(range(heads))):
        block = pl.ds(first, 2 * rows)
        if masked:
            col = lax.broadcasted_iota(jnp.int32, (1, 4 * rows), 1)
            row = lax.broadcasted_iota(jnp.int32, (2 * rows, 1), 0)
            own = half * rows
            far = (1 - half) * rows
            kpos = jnp.where(
                col < 2 * rows,
                -1,
                jnp.where(col < 3 * rows, col - 2 * rows + own, col - 3 * rows + far),
            )
            qpos = jnp.where(row < rows, row + own, row - rows + far)
        for h in some:
            lanes = pl.ds(h * HEAD_DIM, HEAD_DIM)
            s = lax.dot_general(
                q[block, lanes],
                k[:, lanes],
                (((1,), (1,)), ((), ())),
                preferred_element_type=F32,
            )
            s = s * (scale_ref[0, h] * (LOG2E / math.sqrt(HEAD_DIM)))
            if masked:
                s = jnp.where(kpos <= qpos, s, -jnp.inf)
            e = jnp.exp2(s - jnp.max(s, axis=-1, keepdims=True))
            p = (e * (1.0 / jnp.sum(e, axis=-1, keepdims=True))).astype(BF16)
            o[block, lanes] = jnp.dot(p, v[:, lanes], preferred_element_type=F32).astype(BF16)

    tiles = 4
    span = width // tiles

    def part_copy(which, t):
        send, got = parts[which]
        cols = pl.ds(pl.multiple_of(t * span, span), span)
        return pltpu.make_async_remote_copy(
            src_ref=send.at[:, cols],
            dst_ref=got.at[:, cols],
            send_sem=part_ssem.at[which * tiles + t],
            recv_sem=part_rsem.at[which * tiles + t],
            device_id={"section": mate},
            device_id_type=MESH,
        )

    def back(o, base, which):
        @pl.loop(0, tiles)
        def _(t):
            cols = pl.ds(pl.multiple_of(t * span, span), span)
            both = jnp.dot(
                o[pl.ds(base, 2 * rows), :], wo[:, cols], preferred_element_type=F32
            ).astype(BF16)
            parts[which][0][:, cols] = both[rows:]
            kept[which][:, cols] = both[:rows]
            part_copy(which, t).start()

    def summed(which, finish, after=None):
        @pl.loop(0, tiles)
        def _(t):
            cols = pl.ds(pl.multiple_of(t * span, span), span)
            part_copy(which, t).wait_recv()
            finish(cols, kept[which][:, cols].astype(F32) + parts[which][1][:, cols].astype(F32))
            if after is not None:
                after(t)

    def token_finish(x, dst):
        def finish(cols, total):
            dst[:, cols] = (x[:, cols].astype(F32) + total).astype(BF16)

        return finish

    def state_finish(c, dst):
        def finish(cols, total):
            r = keep[pl.ds(layer, 1), cols]
            dst[:, cols] = (r * c[:, cols].astype(F32) + (1.0 - r) * total).astype(BF16)

        return finish

    loads[0].wait()
    loads[2].wait()
    loads[1].wait()
    loads[3].wait()
    for load in loads[6:]:
        load.start()
    norm_into(c1, mgain, u1, 0)
    norm_into(x1, wgain, u1, 2 * rows)
    pl.semaphore_wait(barrier, n_layers + 2)
    send_u1s = to_mate(u1.at[pl.ds(0, rows)], u1.at[pl.ds(rows, rows)], 0)
    send_u1s.start()
    send_u1t = to_mate(u1.at[pl.ds(2 * rows, rows)], u1.at[pl.ds(3 * rows, rows)], 1)
    send_u1t.start()
    send_c = to_seg(c1, c2, 0)
    send_c.start()

    loads[4].wait()
    vocab = table.shape[0]
    ids = jnp.broadcast_to(codes[...].astype(F32), (HEAD_DIM, 2 * rows)).T
    lane = lax.broadcasted_iota(jnp.int32, ids.shape, 1) + pos * vocab
    for b in range(vocab // HEAD_DIM):
        hit = ids == (lane + b * HEAD_DIM).astype(F32)
        onehot[:, b * HEAD_DIM : (b + 1) * HEAD_DIM] = jnp.where(hit, 1.0, 0.0).astype(BF16)
    loads[5].wait()
    own_rows = pl.ds(pl.multiple_of(half * rows, rows), rows)
    far_rows = pl.ds(pl.multiple_of((1 - half) * rows, rows), rows)

    @pl.loop(0, n_layers)
    def _(j):
        cols = pl.ds(pl.multiple_of(j * chunk, chunk), chunk)
        part = table[:, cols]
        emb_send[j] = jnp.dot(onehot[far_rows, :], part, preferred_element_type=F32).astype(BF16)
        emb_own[j] = jnp.dot(onehot[own_rows, :], part, preferred_element_type=F32).astype(BF16)

    send_emb = to_mate(emb_send, emb_got, 2)
    send_emb.start()

    send_u1s.wait_recv()
    loads[6].wait()
    loads[7].wait()
    loads[8].wait()
    project(u1, 0)

    send_emb.wait_recv()
    emb_own[...] = emb_own[...] + emb_got[...]

    def a2a_copy(step):
        peer = lax.rem(layer + step, n_layers)
        return pltpu.make_async_remote_copy(
            src_ref=emb_own.at[peer],
            dst_ref=a2a.at[layer],
            send_sem=a2a_send.at[peer],
            recv_sem=a2a_recv.at[layer],
            device_id={"section": peer * 2 + half},
            device_id_type=MESH,
        )

    def a2a_arrival(step):
        peer = lax.rem(layer + step, n_layers)
        return pltpu.make_async_remote_copy(
            src_ref=emb_own.at[layer],
            dst_ref=a2a.at[peer],
            send_sem=a2a_send.at[layer],
            recv_sem=a2a_recv.at[peer],
            device_id={"section": peer * 2 + half},
            device_id_type=MESH,
        )

    @pl.loop(1, n_layers)
    def _(step):
        a2a_copy(step).start()

    send_u1t.wait_recv()
    project(u1, 2 * rows)

    attend(o1, 2 * rows, True)
    loads[10].wait()
    back(o1, 2 * rows, 0)

    last = n_layers - 1
    up = jnp.where(layer < last, pos + 2, pos - 2 * last)
    upper = rows // 2

    def token_copy(row, cols, i):
        return pltpu.make_async_remote_copy(
            src_ref=y1.at[pl.ds(row, upper), cols],
            dst_ref=x2.at[pl.ds(row, upper), cols],
            send_sem=tok_send.at[i],
            recv_sem=tok_recv.at[i],
            device_id={"section": up},
            device_id_type=MESH,
        )

    def upper_copy(t):
        return token_copy(0, pl.ds(pl.multiple_of(t * span, span), span), t)

    def lower_copy():
        return token_copy(upper, pl.ds(0, width), tiles)

    def send_tile(t):
        @pl.when(layer < last)
        def _():
            upper_copy(t).start()

    def send_heads(i):
        lanes = pl.ds(i * (heads // 2) * HEAD_DIM, (heads // 2) * HEAD_DIM)
        copy = to_seg(o1.at[pl.ds(0, 2 * rows), lanes], ost.at[:, lanes], 1 + i)
        copy.start()
        return copy

    attend(o1, 0, False, range(heads // 2))
    send_o0 = send_heads(0)
    summed(0, token_finish(x1, y1), send_tile)

    @pl.when(layer < last)
    def _():
        lower_copy().start()

    attend(o1, 0, False, range(heads // 2, heads))
    send_o1 = send_heads(1)

    emb_red[...] = emb_own[layer]

    @pl.loop(1, n_layers)
    def _(step):
        a2a_arrival(step).wait_recv()
        emb_red[...] = emb_red[...] + a2a[lax.rem(layer + step, n_layers)]

    my_cols = pl.ds(pl.multiple_of(layer * chunk, chunk), chunk)

    def red_copy():
        return pltpu.make_async_remote_copy(
            src_ref=emb_red,
            dst_ref=x2.at[:, my_cols],
            send_sem=red_send,
            recv_sem=red_recv.at[layer],
            device_id={"section": half},
            device_id_type=MESH,
        )

    @pl.when(layer > 0)
    def _():
        red_copy().start()

    send_o0.wait_recv()
    send_o1.wait_recv()
    back(ost, 0, 1)
    send_c.wait_recv()
    loads[9].wait()
    summed(1, state_finish(c2, s2))
    norm_into(s2, mgain, u2, 0)
    send_u2s = to_mate(u2.at[pl.ds(0, rows)], u2.at[pl.ds(rows, rows)], 3)
    send_u2s.start()
    send_u2s.wait_recv()
    project(u2, 0)

    @pl.when(layer > 0)
    def _():
        @pl.loop(0, tiles)
        def _(t):
            upper_copy(t).wait_recv()

    @pl.when(layer == 0)
    def _():
        x2[:, 0:chunk] = emb_red[...]

        @pl.loop(1, n_layers)
        def _(i):
            cols = pl.ds(pl.multiple_of(i * chunk, chunk), chunk)
            pltpu.make_async_remote_copy(
                src_ref=emb_red,
                dst_ref=x2.at[:, cols],
                send_sem=red_send,
                recv_sem=red_recv.at[i],
                device_id={"section": mate},
                device_id_type=MESH,
            ).wait_recv()

    norm_into(x2, wgain, u2, 2 * rows, 0, upper)
    send_u2a = to_mate(u2.at[pl.ds(2 * rows, upper)], u2.at[pl.ds(3 * rows, upper)], 4)
    send_u2a.start()

    @pl.when(layer > 0)
    def _():
        lower_copy().wait_recv()

    norm_into(x2, wgain, u2, 2 * rows, upper, upper)
    send_u2b = to_mate(
        u2.at[pl.ds(2 * rows + upper, upper)], u2.at[pl.ds(3 * rows + upper, upper)], 5
    )
    send_u2b.start()
    send_u2a.wait_recv()
    send_u2b.wait_recv()
    project(u2, 2 * rows)

    attend(o2, 2 * rows, True)
    back(o2, 2 * rows, 2)
    attend(o2, 0, False)
    back(o2, 0, 3)
    summed(2, token_finish(x2, fin_tok))
    write_tok = pltpu.make_async_copy(fin_tok, tok_out, out_sem.at[0])
    write_tok.start()
    summed(3, state_finish(s2, fin_st))
    write_st = pltpu.make_async_copy(fin_st, st_out, out_sem.at[1])
    write_st.start()

    for copy in (
        send_u1s,
        send_u1t,
        send_c,
        send_emb,
        send_o0,
        send_o1,
        send_u2s,
        send_u2a,
        send_u2b,
    ):
        copy.wait_send()

    @pl.loop(1, n_layers)
    def _(step):
        a2a_copy(step).wait_send()

    for which in range(len(parts)):

        @pl.loop(0, tiles)
        def _(t, which=which):
            part_copy(which, t).wait_send()

    @pl.when(layer < last)
    def _():
        @pl.loop(0, tiles)
        def _(t):
            upper_copy(t).wait_send()

        lower_copy().wait_send()

    @pl.when(layer > 0)
    def _():
        red_copy().wait_send()

    write_tok.wait()
    write_st.wait()


def write_kernel(tok_in, st_in, tok_out, st_out, held, in_sems, out_sems):
    ends = ((tok_in, tok_out), (st_in, st_out))
    reads = [pltpu.make_async_copy(a, held.at[i], in_sems.at[i]) for i, (a, _) in enumerate(ends)]
    writes = [pltpu.make_async_copy(held.at[i], b, out_sems.at[i]) for i, (_, b) in enumerate(ends)]
    for read in reads:
        read.start()
    for read, write in zip(reads, writes):
        read.wait()
        write.start()
    for write in writes:
        write.wait()


def per_device(n_layers, n_seg, codes, table, tok, st, wq, wk, wv, wo, wgain, mgain, keep, scale):
    rows, width = tok.shape[1:]
    inner = wq.shape[2]
    vocab = table.shape[0]
    chunk = width // n_layers
    any_spec = pl.BlockSpec(memory_space=pl.ANY)
    act = pltpu.VMEM((rows, width), BF16)
    big = pltpu.VMEM((4 * rows, width), BF16)
    mid = pltpu.VMEM((4 * rows, inner), BF16)
    emb = pltpu.VMEM((n_layers, rows, chunk), BF16)
    gain = pltpu.VMEM(wgain.shape, F32)
    sem = pltpu.SemaphoreType.DMA
    tok_new, st_new = pl.pallas_call(
        functools.partial(cell_kernel, n_layers, n_seg),
        out_shape=(jax.ShapeDtypeStruct((rows, width), BF16),) * 2,
        in_specs=[any_spec] * 11 + [pl.BlockSpec(memory_space=pltpu.SMEM)],
        out_specs=(any_spec, any_spec),
        scratch_shapes=[
            pltpu.VMEM(codes.shape, jnp.int32),
            pltpu.VMEM((vocab, width), BF16),
            act,
            act,
            pltpu.VMEM((width, inner), BF16),
            pltpu.VMEM((width, inner), BF16),
            pltpu.VMEM((width, inner), BF16),
            pltpu.VMEM((inner, width), BF16),
            gain,
            gain,
            gain,
            pltpu.VMEM((codes.shape[1], vocab), BF16),
            emb,
            emb,
            emb,
            emb,
            pltpu.VMEM((rows, chunk), BF16),
            big,
            big,
            mid,
            mid,
            mid,
            mid,
            mid,
            pltpu.VMEM((2 * rows, inner), BF16),
        ]
        + [act] * 18
        + [
            sem((11,)),
            sem((6,)),
            sem((6,)),
            sem((16,)),
            sem((16,)),
            sem((n_layers,)),
            sem((n_layers,)),
            sem,
            sem((n_layers,)),
            sem((3,)),
            sem((3,)),
            sem((5,)),
            sem((5,)),
            sem((2,)),
        ],
        compiler_params=pltpu.CompilerParams(
            collective_id=0, has_side_effects=True, vmem_limit_bytes=58 * 1024 * 1024
        ),
    )(
        codes,
        table,
        tok[0],
        st[0],
        wq[0],
        wk[0],
        wv[0],
        wo[0],
        wgain,
        mgain,
        keep,
        scale,
    )
    tok_new, st_new = pl.pallas_call(
        write_kernel,
        out_shape=(jax.ShapeDtypeStruct((rows, width), BF16),) * 2,
        in_specs=[any_spec, any_spec],
        out_specs=(any_spec, any_spec),
        scratch_shapes=[pltpu.VMEM((2, rows, width), BF16), sem((2,)), sem((2,))],
    )(tok_new, st_new)
    return (tok_new[None], st_new[None])


def solution(mesh):
    placed = (
        P("seg", None),
        P("section", None),
        P("seg", "section", None),
        P("seg", "section", None),
        P("section", None, None),
        P("section", None, None),
        P("section", None, None),
        P("section", None, None),
        P(),
        P(),
        P(),
        P("section", None),
    )
    return jax.shard_map(
        functools.partial(per_device, mesh.shape["section"] // 2, mesh.shape["seg"]),
        mesh=mesh,
        in_specs=placed,
        out_specs=(P("seg", "section", None), P("seg", "section", None)),
        check_vma=False,
    )
```
